32 devices in a mesh: dp: 2 (over core), row: 4 (over z), col: 4 (over y, x).
Axes of the slice: x: 2, y: 2, z: 4, core: 2. Of those that a mesh axis runs over, the one named last changes fastest.
Arguments:
- grad_in: bfloat16 [2, 4096, 16384], P('dp', 'row', 'col'), may hold values from -50 to 50
- grad_out: bfloat16 [2, 16384, 4096], P('dp', 'row', 'col'), may hold values from -50 to 50
- rows_in: float32 [4096], P('row'), may hold values from 0.05 to 0.5
- cols_in: float32 [16384], P('col'), may hold values from 0.05 to 0.5
- rows_out: float32 [16384], P('row'), may hold values from 0.05 to 0.5
- cols_out: float32 [4096], P('col'), may hold values from 0.05 to 0.5
Outputs:
- update_in: float32 [4096, 16384], P('row', 'col')
- update_out: float32 [16384, 4096], P('row', 'col')
- rows_in_new: float32 [4096], P('row')
- cols_in_new: float32 [16384], P('col')
- rows_out_new: float32 [16384], P('row')
- cols_out_new: float32 [4096], P('col')
The draws below stay inside these ranges and needn't reach their ends.
All inputs are finite; a program needn't handle non-finite values.
Results may differ from the reference program's by a relative error of at most 0.00045.
Values sent between devices are 32-bit elements; how exact they have to be, the bound alone decides.
A program may use at most 128 MiB of HBM per device.

```python
import math
import jax
import jax.numpy as jnp
from jax import lax

D = 4096
FF = 16384
REPLICAS = 2


def draw_parts(key, height, width):
    key_rows, key_cols, key_noise = jax.random.split(key, 3)
    rise_rows = jnp.arange(height, dtype=jnp.float32) / (height - 1)
    rise_cols = jnp.arange(width, dtype=jnp.float32) / (width - 1)
    row_scale = 10.0 ** (0.5 * jax.random.uniform(key_rows, (height,)) + 0.5 * rise_rows)
    col_scale = 10.0 ** (0.5 * jax.random.uniform(key_cols, (width,)) + 0.5 * rise_cols)
    noise = jnp.clip(jax.random.normal(key_noise, (REPLICAS, height, width)), -5.0, 5.0)
    return 0.1 * noise * row_scale[None, :, None] * col_scale[None, None, :]


def draw_grad_in(key, part):
    key = jax.random.fold_in(key, 1)
    return draw_parts(key, D, FF).astype(jnp.bfloat16)


def draw_grad_out(key, part):
    key = jax.random.fold_in(key, 2)
    return draw_parts(key, FF, D).astype(jnp.bfloat16)


def level_of(rng, extent, cuts, low, high):
    def one(axis_at, blocks):
        heights = jax.random.uniform(jax.random.fold_in(jax.random.fold_in(rng, 6), axis_at), (blocks,), jnp.float32, low / len(cuts), high / len(cuts))
        return jnp.repeat(jnp.exp(heights), extent[axis_at] // blocks).reshape((-1,) + (1,) * (len(extent) - axis_at - 1))

    loudness = one(*cuts[0])
    for cut in cuts[1:]:
        loudness = loudness * one(*cut)
    return loudness


def setup_inputs(seed: int = 0) -> dict:
    arg_keys = jax.random.split(jax.random.key(seed), 7)
    return {
        "grad_in": draw_grad_in(jax.random.fold_in(arg_keys[6], 71), 0),
        "grad_out": draw_grad_out(jax.random.fold_in(arg_keys[6], 71), 0),
        "rows_in": jnp.clip(jnp.exp(math.log(0.5) - 2.3025851 * jax.random.uniform(arg_keys[2], (D,), jnp.float32) ** level_of(arg_keys[2], (D,), ((0, 4),), -0.2, 0.2)), 0.05, 0.5),
        "cols_in": jnp.clip(jnp.exp(math.log(0.5) - 2.3025851 * jax.random.uniform(arg_keys[3], (FF,), jnp.float32) ** level_of(arg_keys[3], (FF,), ((0, 4),), -0.2, 0.2)), 0.05, 0.5),
        "rows_out": jnp.clip(jnp.exp(math.log(0.5) - 2.3025851 * jax.random.uniform(arg_keys[4], (FF,), jnp.float32) ** level_of(arg_keys[4], (FF,), ((0, 4),), -0.2, 0.2)), 0.05, 0.5),
        "cols_out": jnp.clip(jnp.exp(math.log(0.5) - 2.3025851 * jax.random.uniform(arg_keys[5], (D,), jnp.float32) ** level_of(arg_keys[5], (D,), ((0, 4),), -0.2, 0.2)), 0.05, 0.5),
    }


EPSILON = 1e-30
DECAY = 1.0 - 100.0 ** (-0.8)

def factored(parts, rows_old, cols_old):
    summed = parts[0].astype(jnp.float32)
    for index in range(1, REPLICAS):
        summed = summed + parts[index].astype(jnp.float32)
    squares = summed * summed + EPSILON
    rows_new = DECAY * rows_old + (1.0 - DECAY) * lax.optimization_barrier(jnp.mean(squares, axis=1))
    cols_new = DECAY * cols_old + (1.0 - DECAY) * lax.optimization_barrier(jnp.mean(squares, axis=0))
    scaled = summed * lax.rsqrt(rows_new)[:, None] * lax.rsqrt(cols_new)[None, :]
    ratio = jnp.sqrt(jnp.mean(scaled * scaled))
    update = scaled / jnp.maximum(1.0, ratio)
    return (update, rows_new, cols_new)

def reference(grad_in, grad_out, rows_in, cols_in, rows_out, cols_out):
    update_in, rows_in_new, cols_in_new = factored(grad_in, rows_in, cols_in)
    update_out, rows_out_new, cols_out_new = factored(grad_out, rows_out, cols_out)
    return (update_in, update_out, rows_in_new, cols_in_new, rows_out_new, cols_out_new)
```

```python
import functools
import jax
import jax.numpy as jnp
from jax import lax
from jax.experimental import pallas as pl
from jax.experimental.pallas import tpu as pltpu
from jax.sharding import PartitionSpec as P

EPSILON = 1e-30
DECAY = 1.0 - 100.0 ** (-0.8)
MESH = pl.DeviceIdType.MESH
F32 = jnp.float32
CHUNKS = 8
SLOTS = 3
LAG = 3


def kernel(nr, nc, g_in, g_out, rows_in, cols_in, rows_out, cols_out,
           acc_in, acc_out, rnew_in, cnew_in, rnew_out, cnew_out, rf_in, cf_in, rf_out, cf_out,
           own_in, own_out, oth_in, oth_out, stage_in, stage_out, rowp_in, rowp_out, colp_in, colp_out,
           rrep_in, rrep_out, rowsend, rowrecv, colsend, colrecv, esend, erecv, fsend, frecv,
           own_sem, oth_sem, rs_send, rs_recv, ag_send, ag_recv,
           row_s, row_r, col_s, col_r, e_s, e_r, f_s, f_r):
    d, r, c = lax.axis_index("dp"), lax.axis_index("row"), lax.axis_index("col")
    partner = (1 - d, r, c)
    ncol, nrow = 2 * nc, 2 * nr
    my_col, my_row = d * nc + c, d * nr + r

    def col_peer(q):
        p = lax.rem(my_col + q, ncol)
        return (p // nc, r, lax.rem(p, nc))

    def row_peer(q):
        p = lax.rem(my_row + q, nrow)
        return (p // nr, lax.rem(p, nr), c)

    grads, accs = (g_in, g_out), (acc_in, acc_out)
    owns, oths, stages = (own_in, own_out), (oth_in, oth_out), (stage_in, stage_out)
    rowps, colps, rreps = (rowp_in, rowp_out), (colp_in, colp_out), (rrep_in, rrep_out)
    halves = [a.shape[0] // 2 for a in accs]
    chs = [h // CHUNKS for h in halves]
    widths = [a.shape[1] for a in accs]
    tasks = [(m, k) for m in range(2) for k in range(CHUNKS)]
    n = len(tasks)

    def rows_of(m, k, who):
        return pl.ds(pl.multiple_of(who * halves[m] + k * chs[m], chs[m]), chs[m])

    loads_own, loads_oth = [], []
    for t, (m, k) in enumerate(tasks):
        loads_oth.append(pltpu.make_async_copy(
            grads[m].at[0, rows_of(m, k, 1 - d), :], oths[m].at[pl.ds(k * chs[m], chs[m]), :], oth_sem.at[t]))
        loads_own.append(pltpu.make_async_copy(
            grads[m].at[0, rows_of(m, k, d), :], owns[m].at[pl.ds(k * chs[m], chs[m]), :], own_sem.at[t]))
    for t in range(n):
        loads_oth[t].start()
        loads_own[t].start()

    barrier = pltpu.get_barrier_semaphore()
    for q in range(1, ncol):
        pl.semaphore_signal(barrier, inc=1, device_id=col_peer(q), device_id_type=MESH)
    for q in range(1, nrow):
        pl.semaphore_signal(barrier, inc=1, device_id=row_peer(q), device_id_type=MESH)
    for m in range(2):
        colps[m][...] = jnp.zeros_like(colps[m])
    rowsend[...] = jnp.zeros_like(rowsend)
    pl.semaphore_wait(barrier, ncol + nrow - 2)

    rs, rs_in, ag, ag_in = [], [], [], []
    for t, (m, k) in enumerate(tasks):
        rs.append(pltpu.make_async_remote_copy(
            src_ref=stages[m].at[k % SLOTS], dst_ref=accs[m].at[rows_of(m, k, 1 - d), :],
            send_sem=rs_send.at[t], recv_sem=rs_recv.at[t], device_id=partner, device_id_type=MESH))
        rs_in.append(pltpu.make_async_remote_copy(
            src_ref=stages[m].at[k % SLOTS], dst_ref=accs[m].at[rows_of(m, k, d), :],
            send_sem=rs_send.at[t], recv_sem=rs_recv.at[t], device_id=partner, device_id_type=MESH))
        ag.append(pltpu.make_async_remote_copy(
            src_ref=accs[m].at[rows_of(m, k, d), :], dst_ref=accs[m].at[rows_of(m, k, d), :],
            send_sem=ag_send.at[t], recv_sem=ag_recv.at[t], device_id=partner, device_id_type=MESH))
        ag_in.append(pltpu.make_async_remote_copy(
            src_ref=accs[m].at[rows_of(m, k, 1 - d), :], dst_ref=accs[m].at[rows_of(m, k, 1 - d), :],
            send_sem=ag_send.at[t], recv_sem=ag_recv.at[t], device_id=partner, device_id_type=MESH))

    def send(t):
        m, k = tasks[t]
        if k >= SLOTS:
            rs[t - SLOTS].wait_send()
        loads_oth[t].wait()

        @pl.loop(0, chs[m] // 16)
        def _(i):
            at = pl.multiple_of(i * 16, 16)
            src = pl.multiple_of(k * chs[m] + i * 16, 16)
            stages[m][k % SLOTS, pl.ds(at, 16), :] = oths[m][pl.ds(src, 16), :].astype(F32)

        rs[t].start()

    def take(t):
        m, k = tasks[t]
        loads_own[t].wait()
        rs_in[t].wait_recv()
        step = min(1024, widths[m])

        @pl.loop(0, chs[m] // 16)
        def _(i):
            at = pl.multiple_of(k * chs[m] + i * 16, 16)
            there = pl.multiple_of(d * halves[m] + k * chs[m] + i * 16, 16)
            part = jnp.zeros((16, 128), F32)
            for b in range(0, widths[m], step):
                s = accs[m][pl.ds(there, 16), b:b + step] + owns[m][pl.ds(at, 16), b:b + step].astype(F32)
                accs[m][pl.ds(there, 16), b:b + step] = s
                sq = s * s + EPSILON
                colps[m][:, b:b + step] += sq[:8] + sq[8:]
                for j in range(0, step, 128):
                    part = part + sq[:, j:j + 128]
            rowps[m][pl.ds(at, 16), :] = part

    for t in range(n):
        send(t)
        if t >= LAG:
            take(t - LAG)
    for t in range(n - LAG):
        ag[t].start()
    for t in range(n - LAG, n):
        take(t)
        ag[t].start()

    nbs = [h // 128 for h in halves]
    offs = [0, (nbs[0] + 7) // 8 * 8]
    for m in range(2):
        for b in range(nbs[m]):
            rowsend[offs[m] + b:offs[m] + b + 1, :] = jnp.sum(
                rowps[m][b * 128:(b + 1) * 128, :].T, axis=0, keepdims=True)
    colsend[:, :widths[0]] = jnp.sum(colp_in[...], axis=0, keepdims=True)
    colsend[:, widths[0]:] = jnp.sum(colp_out[...], axis=0, keepdims=True)

    def exchange(src, dst, me, count, peer, ssem, rsem):
        copies = []
        for q in range(1, count):
            copies.append((pltpu.make_async_remote_copy(
                src_ref=src, dst_ref=dst.at[me], send_sem=ssem.at[q], recv_sem=rsem.at[q],
                device_id=peer(q), device_id_type=MESH),
                pltpu.make_async_remote_copy(
                src_ref=src, dst_ref=dst.at[lax.rem(me + count - q, count)], send_sem=ssem.at[q],
                recv_sem=rsem.at[q], device_id=peer(q), device_id_type=MESH)))
        for out, _ in copies:
            out.start()
        dst[me] = src[...]
        return copies

    def finish(copies):
        for out, into in copies:
            into.wait_recv()
            out.wait_send()

    row_copies = exchange(rowsend, rowrecv, my_col, ncol, col_peer, row_s, row_r)
    col_copies = exchange(colsend, colrecv, my_row, nrow, row_peer, col_s, col_r)
    finish(row_copies)
    finish(col_copies)

    fulls = [(widths[m] * nc, accs[m].shape[0] * nr) for m in range(2)]
    for m, (old, new, rf) in enumerate(((rows_in, rnew_in, rf_in), (rows_out, rnew_out, rf_out))):
        for h in range(2):
            total = rowrecv[h * nc, offs[m]:offs[m] + nbs[m], :]
            for j in range(1, nc):
                total = total + rowrecv[h * nc + j, offs[m]:offs[m] + nbs[m], :]
            fresh = DECAY * old[h * nbs[m]:(h + 1) * nbs[m], :] + (1.0 - DECAY) * (total / fulls[m][0])
            new[h * nbs[m]:(h + 1) * nbs[m], :] = fresh
            rf[h * nbs[m]:(h + 1) * nbs[m], :] = lax.rsqrt(fresh)
    csum = colrecv[0]
    for j in range(1, nrow):
        csum = csum + colrecv[j]
    for m, (old, new, cf) in enumerate(((cols_in, cnew_in, cf_in), (cols_out, cnew_out, cf_out))):
        total = csum[:, :widths[0]] if m == 0 else csum[:, widths[0]:]
        fresh = DECAY * old[...] + (1.0 - DECAY) * (total / fulls[m][1])
        new[...] = fresh
        cf[...] = lax.rsqrt(fresh)

    for m, (rf, cf) in enumerate(((rf_in, cf_in), (rf_out, cf_out))):
        for b in range(nbs[m]):
            line = rf[pl.ds(d * nbs[m] + b, 1), :]
            rreps[m][b * 128:(b + 1) * 128, :] = jnp.broadcast_to(line, (128, 128)).T

        def body(i, total):
            at = pl.multiple_of(i * 16, 16)
            there = pl.multiple_of(d * halves[m] + i * 16, 16)
            factor = rreps[m][pl.ds(at, 16), :]
            for j in range(0, widths[m], 128):
                x = accs[m][pl.ds(there, 16), j:j + 128] * factor * cf[:, j:j + 128]
                total = total + x * x
            return total

        energy = lax.fori_loop(0, halves[m] // 16, body, jnp.zeros((16, 128), F32))
        esend[m * 8:(m + 1) * 8, :] = energy[:8] + energy[8:]

    finish(exchange(esend, erecv, my_col, ncol, col_peer, e_s, e_r))
    total = erecv[0]
    for j in range(1, ncol):
        total = total + erecv[j]
    fsend[...] = total

    def ring_peer(q):
        return (d, lax.rem(r + q, nr), c)

    finish(exchange(fsend, frecv, r, nr, ring_peer, f_s, f_r))
    total = frecv[0]
    for j in range(1, nr):
        total = total + frecv[j]
    for m, rf in enumerate((rf_in, rf_out)):
        mean = jnp.sum(total[m * 8:(m + 1) * 8, :], keepdims=True) / (float(fulls[m][0]) * fulls[m][1])
        rf[...] = rf[...] * (1.0 / jnp.maximum(1.0, jnp.sqrt(mean)))

    for t, (m, k) in enumerate(tasks):
        if k >= CHUNKS - SLOTS:
            rs[t].wait_send()
        ag_in[t].wait_recv()
        ag[t].wait_send()


def fused(nr, nc, grad_in, grad_out, rows_in, cols_in, rows_out, cols_out):
    (ri, ci), (ro, co) = grad_in.shape[1:], grad_out.shape[1:]
    hi, ho = ri // 2, ro // 2
    nb = (hi // 128 + 7) // 8 * 8 + (ho // 128 + 7) // 8 * 8
    vm = pl.BlockSpec(memory_space=pltpu.VMEM)
    small = lambda *s: jax.ShapeDtypeStruct(s, F32)
    dma = lambda k: pltpu.SemaphoreType.DMA((k,))
    n = 2 * CHUNKS
    vmem = lambda *s: pltpu.VMEM(s, F32)
    outs = pl.pallas_call(
        functools.partial(kernel, nr, nc),
        out_shape=(
            pltpu.VMEM((ri, ci), F32), pltpu.VMEM((ro, co), F32),
            small(ri // 128, 128), small(1, ci), small(ro // 128, 128), small(1, co),
            small(ri // 128, 128), small(1, ci), small(ro // 128, 128), small(1, co),
        ),
        in_specs=[pl.BlockSpec(memory_space=pl.ANY)] * 2 + [vm] * 4,
        out_specs=(vm,) * 10,
        scratch_shapes=[
            pltpu.VMEM((hi, ci), jnp.bfloat16), pltpu.VMEM((ho, co), jnp.bfloat16),
            pltpu.VMEM((hi, ci), jnp.bfloat16), pltpu.VMEM((ho, co), jnp.bfloat16),
            vmem(SLOTS, hi // CHUNKS, ci), vmem(SLOTS, ho // CHUNKS, co),
            vmem(hi, 128), vmem(ho, 128), vmem(8, ci), vmem(8, co),
            vmem(hi, 128), vmem(ho, 128),
            vmem(nb, 128), vmem(2 * nc, nb, 128),
            vmem(1, ci + co), vmem(2 * nr, 1, ci + co),
            vmem(16, 128), vmem(2 * nc, 16, 128), vmem(16, 128), vmem(nr, 16, 128),
            dma(n), dma(n), dma(n), dma(n), dma(n), dma(n),
            dma(2 * nc), dma(2 * nc), dma(2 * nr), dma(2 * nr),
            dma(2 * nc), dma(2 * nc), dma(nr), dma(nr),
        ],
        compiler_params=pltpu.CompilerParams(
            collective_id=0, has_side_effects=True, vmem_limit_bytes=VMEM_LIMIT),
    )(grad_in, grad_out, rows_in.reshape(-1, 128), cols_in.reshape(1, -1),
      rows_out.reshape(-1, 128), cols_out.reshape(1, -1))
    s_in, s_out, rn_in, cn_in, rn_out, cn_out, rf_in, cf_in, rf_out, cf_out = outs
    update_in = s_in * rf_in.reshape(-1)[:, None] * cf_in
    update_out = s_out * rf_out.reshape(-1)[:, None] * cf_out
    return (update_in, update_out, rn_in.reshape(-1), cn_in.reshape(-1), rn_out.reshape(-1), cn_out.reshape(-1))


VMEM_LIMIT = 29 * 1024 * 1024


def plain(nr, nc, grad_in, grad_out, rows_in, cols_in, rows_out, cols_out):
    def one(grad, rows, cols):
        height, width = grad.shape[1] * nr, grad.shape[2] * nc
        summed = lax.psum(grad[0].astype(F32), "dp")
        square = summed * summed + EPSILON
        rows_new = DECAY * rows + (1.0 - DECAY) * (lax.psum(jnp.sum(square, axis=1), "col") / width)
        cols_new = DECAY * cols + (1.0 - DECAY) * (lax.psum(jnp.sum(square, axis=0), "row") / height)
        scaled = summed * lax.rsqrt(rows_new)[:, None] * lax.rsqrt(cols_new)[None, :]
        energy = lax.psum(jnp.sum(scaled * scaled), ("row", "col"))
        ratio = jnp.sqrt(energy / (float(height) * width))
        return scaled / jnp.maximum(1.0, ratio), rows_new, cols_new

    u_in, r_in, c_in = one(grad_in, rows_in, cols_in)
    u_out, r_out, c_out = one(grad_out, rows_out, cols_out)
    return (u_in, u_out, r_in, c_in, r_out, c_out)


def solution(mesh):
    nr, nc = mesh.shape["row"], mesh.shape["col"]

    def per_device(grad_in, grad_out, *factors):
        whole = all(g.shape[1] % (256 * CHUNKS // 4) == 0 and g.shape[2] % 1024 == 0 for g in (grad_in, grad_out))
        return (fused if whole else plain)(nr, nc, grad_in, grad_out, *factors)

    return jax.shard_map(
        per_device,
        mesh=mesh,
        in_specs=(P("dp", "row", "col"), P("dp", "row", "col"), P("row"), P("col"), P("row"), P("col")),
        out_specs=(P("row", "col"), P("row", "col"), P("row"), P("col"), P("row"), P("col")),
        check_vma=False,
    )
```
